512 devices in a mesh: lat: 64 (over y, x, core), lon: 8 (over z).
Axes of the slice: x: 4, y: 8, z: 8, core: 2. Of those that a mesh axis runs over, the one named last changes fastest.
Arguments:
- ensemble: float32 [81, 10, 128, 1024], P(None, None, 'lat', 'lon'), may hold values from -6 to 6
- obs_values: float32 [3, 512], replicated, may hold values from -8 to 8
- obs_errors: float32 [3, 512], replicated, may hold values from 2 to 20
- obs_device: int32 [3, 512], replicated, may hold values from 0 to 511, as said below
- obs_cell: int32 [3, 512], replicated, may hold values from 0 to 2559
- obs_order: int32 [3, 512], replicated, may hold values from 0 to 511, each once within a row
- coupling: int32 [3, 64, 64, 8], P(None, None, 'lat', 'lon'), may hold values 0 or 1
Outputs:
- analysis: float32 [81, 10, 128, 1024], P(None, None, 'lat', 'lon')
The draws below stay inside these ranges and needn't reach their ends.
Inputs may be any that keep to these rules, and one draw needn't show every extreme that they name: `obs_device`: in every batch each state group holds at most 2 observations, and some group holds exactly 2.
All inputs are finite; a program needn't handle non-finite values. No bound on the sum of `coupling` on one device may be relied on, other than what follows from the above.
Results may differ from the reference program's by a relative error of at most 0.0003.
Values sent between devices are 32-bit elements; how exact they have to be, the bound alone decides.
No kernel may reach another device: no remote copies, remote signals or barrier semaphores. Data moves between devices by JAX's collectives and lax.ppermute only.
A program may use at most 64 MiB of HBM per device.

```python
import math
import jax
import jax.numpy as jnp
from jax import lax

AUG = 81
LEV = 10
LATC = 2
LONC = 128
NBATCH = 3
OBLK = 64
OB = 8
NOBS = 512
NDEV = 512
CAP = 2
N_LAT = 64
N_LON = 8


def draw_obs_device(key, part):
    key = jax.random.fold_in(key, 11)

    def single(batch_key):
        key_first, key_slots, key_shuffle = jax.random.split(batch_key, 3)
        busiest = jax.random.randint(key_first, (), 0, NDEV)
        slots = jax.random.permutation(key_slots, (NDEV - 1) * CAP)[:NOBS - CAP]
        others = slots // CAP
        others = others + (others >= busiest).astype(jnp.int32)
        placed = jnp.concatenate([jnp.full((CAP,), busiest, jnp.int32), others.astype(jnp.int32)])
        return jax.random.permutation(key_shuffle, placed)
    return jax.vmap(single)(jax.random.split(key, NBATCH)).astype(jnp.int32)


def place_ends(array, rng, least, high):
    longest = array.shape.index(max(array.shape))
    spots = []
    for shift in (0, 1):
        where = [jax.random.randint(jax.random.fold_in(rng, axis), (), 0, length) for axis, length in enumerate(array.shape)]
        where[longest] = (where[longest] + shift) % array.shape[longest]
        spots.append(tuple(where))
    return array.at[spots[0]].set(least).at[spots[1]].set(high)


def block_levels(key, shape, cuts, smallest, largest):
    level, own = 1.0, jax.random.fold_in(key, 6)
    for dim, blocks in cuts:
        draws = jnp.exp(jax.random.uniform(jax.random.fold_in(own, dim), (blocks,), jnp.float32, smallest / len(cuts), largest / len(cuts)))
        level = level * jnp.repeat(draws, shape[dim] // blocks).reshape([-1 if axis == dim else 1 for axis in range(len(shape))])
    return level


def noise(own_key, dims, width, reach, shards=(), kind=jnp.bfloat16):
    result = width * jax.random.normal(own_key, dims, jnp.float32)
    if shards:
        result = result * block_levels(own_key, dims, shards, -0.22, 0.18)
    return jnp.clip(result, -reach, reach).astype(kind)


def setup_inputs(seed: int = 0) -> dict:
    arg_keys = jax.random.split(jax.random.key(seed), 8)
    return {
        "ensemble": noise(arg_keys[0], (AUG, LEV, LATC * N_LAT, LONC * N_LON), 1.0, 6.0, ((2, 64), (3, 8)), jnp.float32),
        "obs_values": noise(arg_keys[1], (NBATCH, NOBS), 1.5, 8.0, (), jnp.float32),
        "obs_errors": jnp.clip(jnp.exp(jax.random.uniform(arg_keys[2], (NBATCH, NOBS), jnp.float32, math.log(2.0), math.log(20.0))), 2.0, 20.0),
        "obs_device": draw_obs_device(jax.random.fold_in(arg_keys[7], 71), 0),
        "obs_cell": place_ends(jax.random.randint(arg_keys[4], (NBATCH, NOBS), 0, LEV * LATC * LONC), jax.random.fold_in(arg_keys[4], 1), 0, (LEV * LATC * LONC) - 1).astype(jnp.int32),
        "obs_order": jax.vmap(lambda own: jax.random.permutation(own, NOBS))(jax.random.split(arg_keys[5], NBATCH)).reshape((NBATCH, NOBS)).astype(jnp.int32),
        "coupling": place_ends((jax.random.randint(arg_keys[6], (NBATCH, OBLK, N_LAT, N_LON), 0, 4) < 1).astype(jnp.int32), jax.random.fold_in(arg_keys[6], 1), 0, 1),
    }


HIGH = lax.Precision.HIGHEST

def block_maps(prior_rows, block_ids, values, errors):
    augmented = prior_rows.shape[0]
    members = augmented - 1
    count_blocks = block_ids.shape[0]
    priors_start = jnp.transpose(prior_rows[:, block_ids], (1, 2, 0))
    value_blocks = values[block_ids]
    error_blocks = errors[block_ids]
    identity = jnp.eye(augmented, dtype=jnp.float32)
    identity_stack = jnp.broadcast_to(identity, (count_blocks, augmented, augmented))

    def assimilate(position, product):
        column = lax.dynamic_index_in_dim(priors_start, position, 1, keepdims=False)
        error_now = lax.dynamic_index_in_dim(error_blocks, position, 1, keepdims=False)
        value_now = lax.dynamic_index_in_dim(value_blocks, position, 1, keepdims=False)
        prior = jnp.einsum('bij,bj->bi', product, column, precision=HIGH)
        perturb = prior[:, 1:]
        spread = lax.optimization_barrier(jnp.sum(perturb * perturb, axis=1)) / (members - 1)
        denominator = spread + error_now
        factor_gain = 1.0 / ((members - 1) * denominator)
        shrink = 1.0 / (1.0 + jnp.sqrt(error_now / denominator))
        innovation = value_now - prior[:, 0]
        row_mix = jnp.einsum('bi,bij->bj', perturb, product[:, 1:, :], precision=HIGH)
        column_mix = jnp.concatenate([(factor_gain * innovation)[:, None], -(shrink * factor_gain)[:, None] * perturb], axis=1)
        return product + column_mix[:, :, None] * row_mix[:, None, :]
    return lax.fori_loop(0, block_ids.shape[1], assimilate, identity_stack)

def compose(transforms, coupled_row):
    augmented = transforms.shape[1]
    identity = jnp.eye(augmented, dtype=jnp.float32)
    chosen = jnp.where(coupled_row[:, None, None] > 0, transforms, identity[None])
    while chosen.shape[0] > 1:
        chosen = jnp.einsum('kij,kjl->kil', chosen[1::2], chosen[0::2], precision=HIGH)
    return chosen[0]

def reference(ensemble, obs_values, obs_errors, obs_device, obs_cell, obs_order, coupling):
    augmented, levels, rows_all, cols_all = ensemble.shape
    rows_dev = rows_all // N_LAT
    cols_dev = cols_all // N_LON
    device_blocks = ensemble.reshape(augmented, levels, N_LAT, rows_dev, N_LON, cols_dev)
    device_blocks = device_blocks.transpose(2, 4, 0, 1, 3, 5).reshape(N_LAT * N_LON, augmented, levels * rows_dev * cols_dev)
    coupled = coupling.transpose(0, 2, 3, 1).reshape(NBATCH, N_LAT * N_LON, OBLK)
    for batch in range(NBATCH):
        prior_rows = device_blocks[obs_device[batch], :, obs_cell[batch]].T
        block_ids = obs_order[batch].reshape(OBLK, OB)
        transforms = block_maps(prior_rows, block_ids, obs_values[batch], obs_errors[batch])

        def advance(element):
            members_block, coupled_row = element
            return jnp.dot(compose(transforms, coupled_row), members_block, precision=HIGH)
        device_blocks = lax.map(advance, (device_blocks, coupled[batch]))
    analysis = device_blocks.reshape(N_LAT, N_LON, augmented, levels, rows_dev, cols_dev)
    analysis = analysis.transpose(2, 3, 0, 4, 1, 5).reshape(augmented, levels, rows_all, cols_all)
    return analysis
```

```python
import functools
import jax
import jax.numpy as jnp
from jax import lax
from jax.experimental import pallas as pl
from jax.experimental.pallas import tpu as pltpu
from jax.sharding import Mesh, PartitionSpec as P

AUG = 81
NB = 3
NOBS = 512
NBLK = 64
OB = 8
PAY = 640
TAIL = 128 - AUG
F32 = jnp.float32
BF16 = jnp.bfloat16
GR = 128
VMEM_LIMIT = 56 * 1024 * 1024


def split(x):
    hi = x.astype(BF16)
    lo = (x - hi.astype(F32)).astype(BF16)
    return hi, lo


def dot_nn(a, b):
    return lax.dot_general(a, b, (((1,), (0,)), ((), ())), preferred_element_type=F32)


def dot_nt(a, b):
    return lax.dot_general(a, b, (((1,), (1,)), ((), ())), preferred_element_type=F32)


def iota(shape, dim):
    return lax.broadcasted_iota(jnp.int32, shape, dim)


def index_kernel(core_ref, order_ref, device_ref, values_ref, errors_ref, out_ref):
    core = core_ref[0]
    rows = 128
    lane = iota((rows, NOBS), 1)
    for t in range(NB):
        order = order_ref[t:t + 1, :].astype(F32)
        device = device_ref[t:t + 1, :]
        device_f = device.astype(F32)
        slot = jnp.zeros((1, NOBS), F32)
        for part in range(NOBS // rows):
            sub = iota((rows, NOBS), 0) + part * rows
            own = jnp.sum(jnp.where(sub == lane, device_f, 0.0), axis=1, keepdims=True)
            same = jnp.where((own == device_f) & (sub < lane), 1.0, 0.0)
            slot = slot + jnp.sum(same, axis=0, keepdims=True)
        half = ((device >> 3) & 1) ^ core
        place = half * 256 + (device >> 4) * 8 + (device & 7)
        place = place.astype(F32) + slot * 512.0
        values = values_ref[t:t + 1, :]
        errors = errors_ref[t:t + 1, :]
        for part in range(NOBS // rows):
            sub = iota((rows, NOBS), 0) + part * rows
            source = (sub & 63) * OB + (sub >> 6)
            ident = jnp.sum(jnp.where(source == lane, order, 0.0), axis=1, keepdims=True)
            hot = ident == lane.astype(F32)
            for c, table in enumerate((place, values, errors)):
                col = jnp.sum(jnp.where(hot, table, 0.0), axis=1, keepdims=True)
                out_ref[part * rows:(part + 1) * rows, t * 3 + c:t * 3 + c + 1] = col


def main_kernel(own_ref, other_ref, info_ref, coupling_ref, out_ref,
                buf_ref, z_ref, x_ref, r_ref, mask_ref, w_ref, vt_ref, wk_ref, vk_ref,
                vx_ref, sx_ref, wst_ref, vv_ref):
    lanes = iota((64, 128), 1)
    first = lanes == 0
    valid = lanes < AUG

    for t in range(NB):
        for part, ref in ((0, own_ref), (256, other_ref)):
            if t < 2:
                pieces = [ref[:, 256 * t:256 * t + 128], ref[:, 256 * t + 128:256 * t + 256]]
            else:
                lane = iota((256, 128), 1)
                head = pltpu.roll(ref[:, 0:128], 128 - AUG, 1)
                tail = pltpu.roll(ref[:, 128:256], 256 - 2 * AUG + TAIL - (128 - AUG), 1)
                pieces = [ref[:, 512:640], jnp.where(lane < TAIL, head, tail)]
            for s in range(2):
                hi, lo = split(pieces[s])
                buf_ref[s * 512 + part:s * 512 + part + 256, 0:128] = hi
                buf_ref[s * 512 + part:s * 512 + part + 256, 128:256] = lo
            if t == 0:
                lane = iota((256, 128), 1)
                c0 = pltpu.roll(ref[:, 256:384], 128 - AUG, 1)
                c1 = pltpu.roll(ref[:, 384:512], 128 - AUG + TAIL, 1)
                c2 = pltpu.roll(ref[:, 512:640], (128 - AUG + 2 * TAIL) % 128, 1)
                flags = jnp.where(lane < TAIL, c0, jnp.where(lane < 2 * TAIL, c1, c2)).astype(BF16)
                buf_ref[part:part + 256, 256:384] = flags
                buf_ref[512 + part:512 + part + 256, 256:384] = flags
        width = 256 if t == 0 else 384
        for i in range(4):
            rows = slice(i * 128, (i + 1) * 128)
            place = info_ref[rows, 3 * t:3 * t + 1].astype(jnp.int32)
            hot = jnp.where(place == iota((128, 1024), 1), 1.0, 0.0).astype(BF16)
            got = dot_nn(hot, buf_ref[:, 0:width])
            z = jnp.where(iota((128, 128), 1) < AUG, got[:, 0:128] + got[:, 128:256], 0.0)
            if t == 0:
                z_ref[rows, :] = z
            else:
                at = (0, 640, 128)[t] + i * 128
                x_ref[:, at:at + 128] = z.T
                mask_ref[:, at:at + 128] = got[:, 256:384].T
    x_ref[:, 0:128] = jnp.where((iota((128, 128), 0) == iota((128, 128), 1))
                                    & (iota((128, 128), 0) < AUG), 1.0, 0.0)

    for t in range(NB):
        n = (1152, 640, 128)[t]
        zs = [z_ref[i * 64:(i + 1) * 64, :] for i in range(OB)]
        hs, vs, ws = [], [], []
        for i in range(OB):
            p = zs[i]
            value = info_ref[i * 64:(i + 1) * 64, 3 * t + 1:3 * t + 2]
            error = info_ref[i * 64:(i + 1) * 64, 3 * t + 2:3 * t + 3]
            h = jnp.where(first, 0.0, p)
            q = jnp.sum(h * h, axis=1, keepdims=True) / (AUG - 2) + error
            c = 1.0 / ((AUG - 2) * q)
            a = 1.0 / (1.0 + jnp.sqrt(error / q))
            v = jnp.where(first, c * (value - p[:, 0:1]), -(a * c) * h)
            v = jnp.where(valid, v, 0.0)
            for j in range(i + 1, OB):
                zs[j] = zs[j] + v * jnp.sum(h * zs[j], axis=1, keepdims=True)
            w = h
            for l in range(i):
                w = w + ws[l] * jnp.sum(h * vs[l], axis=1, keepdims=True)
            vs.append(v)
            ws.append(w)
            w_ref[i * 64:(i + 1) * 64, :] = w
            vt_ref[i * 64:(i + 1) * 64, :] = v
        for k in range(NBLK):
            wk_ref[k * 8:k * 8 + 8, :] = w_ref[pl.ds(k, 8, stride=64), :]
            vk_ref[k * 8:k * 8 + 8, :] = vt_ref[pl.ds(k, 8, stride=64), :]
        w_hi, w_lo = split(wk_ref[...])
        w_hh = jnp.concatenate([w_hi, w_hi], axis=1)
        for c in range(0, n, 256):
            c = slice(c, min(c + 256, n))
            x_hi, x_lo = split(x_ref[:, c])
            r_ref[:, c] = dot_nn(w_hh, jnp.concatenate([x_hi, x_lo], axis=0)) + dot_nn(w_lo, x_hi)
        for g in range(4):
            vv_ref[:, g * 128:g * 128 + 128] = vk_ref[g * 128:g * 128 + 128, :].T
        own = jnp.sum(jnp.where(iota((64, 64), 0) == iota((64, 64), 1),
                                coupling_ref[t:t + 1, :].astype(F32), 0.0), axis=1, keepdims=True)
        mask_ref[64 * (t % 2):64 * (t % 2) + 64, 0:128] = jnp.broadcast_to(own, (64, 128))

        for g in range(NOBS // GR):
            lo_row = g * GR
            rows = slice(lo_row, lo_row + GR)
            vg = vk_ref[rows, :]
            v_hi, v_lo = split(vg)
            v_hl = jnp.concatenate([v_hi, v_lo], axis=1)
            wg_hi, wg_lo = w_hi[rows], w_lo[rows]
            bt = dot_nt(v_hl, w_hh[rows]) + dot_nt(v_hi, wg_lo)
            a0 = iota((GR, GR), 0)
            a1 = iota((GR, GR), 1)
            bt = jnp.where(((a0 >> 4) == (a1 >> 4)) & ((a0 & 15) < 8) & ((a1 & 15) >= 8), bt, 0.0)
            b_hi, b_lo = split(bt)
            v12 = dot_nn(jnp.concatenate([b_hi, b_hi], axis=1),
                         jnp.concatenate([v_hi, v_lo], axis=0)) + dot_nn(b_lo, v_hi)
            zero8 = jnp.zeros((8, 128), F32)
            for q in range(GR // 16):
                piece = jnp.concatenate([vg[16 * q:16 * q + 8], vg[16 * q + 8:16 * q + 16],
                                         v12[16 * q:16 * q + 8], zero8], axis=0)
                for rep in range(4):
                    vx_ref[q * 128 + rep * 32:q * 128 + rep * 32 + 32, :] = piece
            e_hi, e_lo = split(vx_ref[...])
            sx = dot_nt(w_hh[rows], jnp.concatenate([e_hi, e_lo], axis=1)) + dot_nt(wg_lo, e_hi)
            s_hi, s_lo = split(sx)
            i0 = iota((GR, 1024), 0)
            i1 = iota((GR, 1024), 1)
            ahead = (i0 >> 4) - (i1 >> 7)
            keep = (ahead > 0) | ((ahead == 0) & ((i0 & 15) >= 8) & ((i1 & 31) < 8))
            sx = jnp.where((i1 & 127) < 64, s_hi.astype(F32), s_lo.astype(F32))
            sx_ref[...] = jnp.where(keep, sx, 0.0).astype(BF16)
            later = NOBS - lo_row - GR
            g_hi, g_lo = split(vv_ref[:, rows])
            if later:
                sg = dot_nt(w_hh[lo_row + GR:], v_hl) + dot_nt(w_lo[lo_row + GR:], v_hi)
                sg_hi, sg_lo = split(sg)
                g_hi = jnp.concatenate([sg_hi, g_hi], axis=0)
                g_lo = jnp.concatenate([sg_lo, g_lo], axis=0)

            chunks = [slice(c, min(c + 256, n)) for c in range(0, n, 256)]
            for q in range(GR // 16):
                top = lo_row + 16 * q
                mrow = 64 * (t % 2) + top // 8
                lhs = sx_ref[16 * q:GR, q * 128:q * 128 + 96]
                for c in chunks:
                    m1 = mask_ref[mrow:mrow + 1, c]
                    m2 = mask_ref[mrow + 1:mrow + 2, c]
                    r1 = r_ref[top:top + 8, c] * m1
                    r2 = r_ref[top + 8:top + 16, c] * m2
                    e = jnp.concatenate([r1, r2, r1 * m2, jnp.zeros_like(r1)], axis=0)
                    e_hi, e_lo = split(e)
                    u = dot_nn(lhs, jnp.concatenate([e_hi, e_lo, e_hi], axis=0))
                    if q < GR // 16 - 1:
                        r_ref[top + 16:lo_row + GR, c] = r_ref[top + 16:lo_row + GR, c] + u[16:]
                    f_hi, f_lo = split(jnp.concatenate([r1, r2 + m2 * u[8:16]], axis=0))
                    wst_ref[16 * q:16 * q + 16, c] = f_hi
                    wst_ref[GR + 16 * q:GR + 16 * q + 16, c] = f_lo
            g_hh = jnp.concatenate([g_hi, g_hi], axis=1)
            for c in [slice(a,a+128) for a in range(0,n,128)]:
                upd = dot_nn(g_hh, wst_ref[:, c]) + dot_nn(g_lo, wst_ref[0:GR, c])
                if later:
                    r_ref[lo_row + GR:, c] = r_ref[lo_row + GR:, c] + upd[0:later]
                x_ref[:, c] = x_ref[:, c] + upd[later:]
        if t < 2:
            for i in range(4):
                at = (640, 128)[t] + i * 128
                z_ref[i * 128:(i + 1) * 128, :] = x_ref[:, at:at + 128].T
    out_ref[...] = x_ref[:, 0:128]


def vmem():
    return pl.BlockSpec(memory_space=pltpu.VMEM)


def index_call(core, order, device, values, errors):
    return pl.pallas_call(
        index_kernel,
        out_shape=jax.ShapeDtypeStruct((NOBS, 128), F32),
        in_specs=[pl.BlockSpec(memory_space=pltpu.SMEM)] + [vmem()] * 4,
        out_specs=vmem(),
        compiler_params=pltpu.CompilerParams(vmem_limit_bytes=VMEM_LIMIT),
        name="positions",
    )(core, order, device, values, errors)


def main_call(own, other, info, coupling):
    return pl.pallas_call(
        main_kernel,
        out_shape=jax.ShapeDtypeStruct((128, 128), F32),
        in_specs=[vmem()] * 4,
        out_specs=vmem(),
        scratch_shapes=[
            pltpu.VMEM((1024, 384), BF16),
            pltpu.VMEM((NOBS, 128), F32),
            pltpu.VMEM((128, 1152), F32),
            pltpu.VMEM((NOBS, 1152), F32),
            pltpu.VMEM((128, 1152), F32),
            pltpu.VMEM((NOBS, 128), F32),
            pltpu.VMEM((NOBS, 128), F32),
            pltpu.VMEM((NOBS, 128), F32),
            pltpu.VMEM((NOBS, 128), F32),
            pltpu.VMEM((1024, 128), F32),
            pltpu.VMEM((GR, 1024), BF16),
            pltpu.VMEM((2 * GR, 1152), BF16),
            pltpu.VMEM((128, NOBS), F32),
        ],
        compiler_params=pltpu.CompilerParams(vmem_limit_bytes=VMEM_LIMIT),
        name="filter",
    )(own, other, info, coupling)


def payload_of(ensemble, device, cell, coupling, me):
    flat = ensemble.reshape(AUG, -1)
    ids = lax.broadcasted_iota(jnp.int32, device.shape, 1)
    found = jnp.where(device == me, ids, NOBS)
    one = jnp.min(found, axis=1, keepdims=True)
    two = jnp.min(jnp.where(found == one, NOBS, found), axis=1, keepdims=True)
    pick = jnp.concatenate([one, two], axis=1)
    hot = pick[:, :, None] == ids[:, None, :]
    place = jnp.sum(jnp.where(hot, cell[:, None, :], 0), axis=2).reshape(-1)
    cols = jnp.where((pick.reshape(-1) < NOBS)[None, :], flat[:, place], 0.0).T
    flags = coupling.reshape(NB, NBLK)[0:2].reshape(-1).astype(F32)
    pad = jnp.zeros((13,), F32)
    return jnp.concatenate([
        cols[0], cols[5, 0:TAIL],
        cols[1], cols[5, TAIL:], pad,
        cols[2], flags[0:TAIL],
        cols[3], flags[TAIL:2 * TAIL],
        cols[4], flags[2 * TAIL:], pad,
    ])


def local(ensemble, obs_values, obs_errors, obs_device, obs_cell, obs_order, coupling):
    core = lax.axis_index("c")
    me = ((lax.axis_index("y") * 4 + lax.axis_index("x")) * 2 + core) * 8 + lax.axis_index("z")
    payload = payload_of(ensemble, obs_device, obs_cell, coupling, me)
    info = index_call(core.reshape(1), obs_order, obs_device, obs_values, obs_errors)
    group = lax.axis_size(("y", "x", "z"))
    own = lax.all_to_all(jnp.broadcast_to(payload[None], (group, PAY)), ("y", "x", "z"), 0, 0)
    other = lax.ppermute(own, "c", [(0, 1), (1, 0)])
    composite = main_call(own, other, info, coupling.reshape(NB, NBLK))
    flat = ensemble.reshape(AUG, -1)
    analysis = jnp.dot(composite[:AUG, :AUG], flat, precision=lax.Precision.HIGHEST)
    return analysis.reshape(ensemble.shape)


def solution(mesh):
    inner = Mesh(mesh.devices.reshape(8, 4, 2, 8), ("y", "x", "c", "z"))
    state = P(None, None, ("y", "x", "c"), "z")
    placed = (state, P(), P(), P(), P(), P(), state)
    return jax.shard_map(local, mesh=inner, in_specs=placed, out_specs=state, check_vma=False)
```

```python
import functools
import jax
import jax.numpy as jnp
from jax import lax
from jax.experimental import pallas as pl
from jax.experimental.pallas import tpu as pltpu
from jax.sharding import Mesh, PartitionSpec as P

AUG = 81
NB = 3
NOBS = 512
NBLK = 64
OB = 8
PAY = 640
TAIL = 128 - AUG
F32 = jnp.float32
BF16 = jnp.bfloat16
GR = 128
XR = 96
WIDE = 128
VMEM_LIMIT = 56 * 1024 * 1024


def split(x):
    hi = x.astype(BF16)
    lo = (x - hi.astype(F32)).astype(BF16)
    return hi, lo


def dot_nn(a, b):
    return lax.dot_general(a, b, (((1,), (0,)), ((), ())), preferred_element_type=F32)


def dot_nt(a, b):
    return lax.dot_general(a, b, (((1,), (1,)), ((), ())), preferred_element_type=F32)


def iota(shape, dim):
    return lax.broadcasted_iota(jnp.int32, shape, dim)


def index_kernel(core_ref, order_ref, device_ref, values_ref, errors_ref, out_ref):
    core = core_ref[0]
    rows = 128
    lane = iota((rows, NOBS), 1)
    for t in range(NB):
        order = order_ref[t:t + 1, :].astype(F32)
        device = device_ref[t:t + 1, :]
        device_f = device.astype(F32)
        slot = jnp.zeros((1, NOBS), F32)
        for part in range(NOBS // rows):
            sub = iota((rows, NOBS), 0) + part * rows
            eye = iota((rows, rows), 0) == iota((rows, rows), 1)
            own = jnp.sum(jnp.where(eye, device_f[:, part * rows:(part + 1) * rows], 0.0), axis=1, keepdims=True)
            same = jnp.where((own == device_f) & (sub < lane), 1.0, 0.0)
            slot = slot + jnp.sum(same, axis=0, keepdims=True)
        half = ((device >> 3) & 1) ^ core
        place = half * 256 + (device >> 4) * 8 + (device & 7)
        place = place.astype(F32) + slot * 512.0
        values = values_ref[t:t + 1, :]
        errors = errors_ref[t:t + 1, :]
        for part in range(NOBS // rows):
            sub = iota((rows, NOBS), 0) + part * rows
            source = (sub & 63) * OB + (sub >> 6)
            ident = jnp.sum(jnp.where(source == lane, order, 0.0), axis=1, keepdims=True)
            hot = ident == lane.astype(F32)
            for c, table in enumerate((place, values, errors)):
                col = jnp.sum(jnp.where(hot, table, 0.0), axis=1, keepdims=True)
                out_ref[part * rows:(part + 1) * rows, t * 3 + c:t * 3 + c + 1] = col


def main_kernel(own_ref, other_ref, info_ref, coupling_ref, out_ref,
                buf_ref, z_ref, x_ref, r_ref, mask_ref, w_ref, vt_ref, wk_ref, vk_ref,
                vx_ref, sx_ref, wst_ref, vv_ref, sh_ref, sl_ref, keep_ref):
    lanes = iota((64, 128), 1)
    first = lanes == 0
    valid = lanes < AUG

    for t in range(NB):
        for part, ref in ((0, own_ref), (256, other_ref)):
            if t < 2:
                pieces = [ref[:, 256 * t:256 * t + 128], ref[:, 256 * t + 128:256 * t + 256]]
            else:
                lane = iota((256, 128), 1)
                head = pltpu.roll(ref[:, 0:128], 128 - AUG, 1)
                tail = pltpu.roll(ref[:, 128:256], 256 - 2 * AUG + TAIL - (128 - AUG), 1)
                pieces = [ref[:, 512:640], jnp.where(lane < TAIL, head, tail)]
            for s in range(2):
                hi, lo = split(pieces[s])
                buf_ref[s * 512 + part:s * 512 + part + 256, 0:128] = hi
                buf_ref[s * 512 + part:s * 512 + part + 256, 128:256] = lo
            if t == 0:
                lane = iota((256, 128), 1)
                c0 = pltpu.roll(ref[:, 256:384], 128 - AUG, 1)
                c1 = pltpu.roll(ref[:, 384:512], 128 - AUG + TAIL, 1)
                c2 = pltpu.roll(ref[:, 512:640], (128 - AUG + 2 * TAIL) % 128, 1)
                flags = jnp.where(lane < TAIL, c0, jnp.where(lane < 2 * TAIL, c1, c2)).astype(BF16)
                buf_ref[part:part + 256, 256:384] = flags
                buf_ref[512 + part:512 + part + 256, 256:384] = flags
        width = 256 if t == 0 else 384
        for i in range(4):
            rows = slice(i * 128, (i + 1) * 128)
            place = info_ref[rows, 3 * t:3 * t + 1].astype(jnp.int32)
            hot = jnp.where(place == iota((128, 1024), 1), 1.0, 0.0).astype(BF16)
            got = dot_nn(hot, buf_ref[:, 0:width])
            z = jnp.where(iota((128, 128), 1) < AUG, got[:, 0:128] + got[:, 128:256], 0.0)
            if t == 0:
                z_ref[rows, :] = z
            else:
                at = (0, 640, 128)[t] + i * 128
                x_ref[:, at:at + 128] = z.T
                mask_ref[:, at:at + 128] = got[:, 256:384].T
    x_ref[:, 0:128] = jnp.where((iota((128, 128), 0) == iota((128, 128), 1))
                                    & (iota((128, 128), 0) < AUG), 1.0, 0.0)

    i0 = iota((GR, 1024), 0)
    i1 = iota((GR, 1024), 1)
    ahead = (i0 >> 4) - (i1 >> 7)
    keep_ref[...] = jnp.where((ahead > 0) | ((ahead == 0) & ((i0 & 15) >= 8) & ((i1 & 31) < 8)), 1.0, 0.0)
    for t in range(NB):
        n = (1152, 640, 128)[t]
        zs = [z_ref[i * 64:(i + 1) * 64, :] for i in range(OB)]
        hs, vs, ws = [], [], []
        for i in range(OB):
            p = zs[i]
            value = info_ref[i * 64:(i + 1) * 64, 3 * t + 1:3 * t + 2]
            error = info_ref[i * 64:(i + 1) * 64, 3 * t + 2:3 * t + 3]
            h = jnp.where(first, 0.0, p)
            q = jnp.sum(h * h, axis=1, keepdims=True) / (AUG - 2) + error
            c = 1.0 / ((AUG - 2) * q)
            a = 1.0 / (1.0 + jnp.sqrt(error / q))
            v = jnp.where(first, c * (value - p[:, 0:1]), -(a * c) * h)
            v = jnp.where(valid, v, 0.0)
            for j in range(i + 1, OB):
                zs[j] = zs[j] + v * jnp.sum(h * zs[j], axis=1, keepdims=True)
            w = h
            for l in range(i):
                w = w + ws[l] * jnp.sum(h * vs[l], axis=1, keepdims=True)
            vs.append(v)
            ws.append(w)
            w_ref[i * 64:(i + 1) * 64, :] = w
            vt_ref[i * 64:(i + 1) * 64, :] = v
        for k in range(NBLK):
            wk_ref[k * 8:k * 8 + 8, :] = w_ref[pl.ds(k, 8, stride=64), :]
            vk_ref[k * 8:k * 8 + 8, :] = vt_ref[pl.ds(k, 8, stride=64), :]
        w_hi, w_lo = split(wk_ref[...])
        w_hh = jnp.concatenate([w_hi, w_hi], axis=1)
        for c in range(0, n, 256):
            c = slice(c, min(c + 256, n))
            x_hi, x_lo = split(x_ref[:, c])
            r_ref[:, c] = dot_nn(w_hh, jnp.concatenate([x_hi, x_lo], axis=0)) + dot_nn(w_lo, x_hi)
        for g in range(4):
            vv_ref[:, g * 128:g * 128 + 128] = vk_ref[g * 128:g * 128 + 128, :].T
        own = jnp.sum(jnp.where(iota((64, 64), 0) == iota((64, 64), 1),
                                coupling_ref[t:t + 1, :].astype(F32), 0.0), axis=1, keepdims=True)
        mask_ref[64 * (t % 2):64 * (t % 2) + 64, 0:128] = jnp.broadcast_to(own, (64, 128))

        vk = vk_ref[...]
        v_hi, v_lo = split(vk)
        v_hl = jnp.concatenate([v_hi, v_lo], axis=1)
        groups = [slice(g * GR, g * GR + GR) for g in range(NOBS // GR)]
        bts = [dot_nt(v_hl[r], w_hh[r]) + dot_nt(v_hi[r], w_lo[r]) for r in groups]
        a0 = iota((GR, GR), 0)
        a1 = iota((GR, GR), 1)
        pairs = ((a0 >> 4) == (a1 >> 4)) & ((a0 & 15) < 8) & ((a1 & 15) >= 8)
        v12s = []
        for r, bt in zip(groups, bts):
            b_hi, b_lo = split(jnp.where(pairs, bt, 0.0))
            v12s.append(dot_nn(jnp.concatenate([b_hi, b_hi], axis=1),
                               jnp.concatenate([v_hi[r], v_lo[r]], axis=0)) + dot_nn(b_lo, v_hi[r]))
        for g in range(NOBS // GR - 1):
            r = groups[g]
            s_hi, s_lo = split(dot_nt(w_hh[r.stop:], v_hl[r]) + dot_nt(w_lo[r.stop:], v_hi[r]))
            sh_ref[r.stop:, r] = s_hi
            sl_ref[r.stop:, r] = s_lo
        zero8 = jnp.zeros((8, 128), F32)
        for g, r in enumerate(groups):
            vg, v12 = vk[r], v12s[g]
            for q in range(GR // 16):
                piece = jnp.concatenate([vg[16 * q:16 * q + 8], vg[16 * q + 8:16 * q + 16],
                                         v12[16 * q:16 * q + 8], zero8], axis=0)
                for rep in range(4):
                    vx_ref[q * 128 + rep * 32:q * 128 + rep * 32 + 32, :] = piece
            e_hi, e_lo = split(vx_ref[...])
            sx = dot_nt(w_hh[r], jnp.concatenate([e_hi, e_lo], axis=1)) + dot_nt(w_lo[r], e_hi)
            sx = sx * keep_ref[...]
            s_hi = sx.astype(BF16).astype(F32)
            sx_ref[r, :] = jnp.where((iota((GR, 1024), 1) & 127) < 64, s_hi, sx - s_hi).astype(BF16)

        chunks = [slice(c, min(c + 256, n)) for c in range(0, n, 256)]
        wide = [slice(c, min(c + WIDE, n)) for c in range(0, n, WIDE)]
        for g, rows in enumerate(groups):
            lo_row = g * GR
            for q in range(GR // 16):
                top = lo_row + 16 * q
                mrow = 64 * (t % 2) + top // 8
                lhs = sx_ref[top:lo_row + GR, q * 128:q * 128 + 96]
                for c in chunks:
                    m1 = mask_ref[mrow:mrow + 1, c]
                    m2 = mask_ref[mrow + 1:mrow + 2, c]
                    r1 = r_ref[top:top + 8, c] * m1
                    r2 = r_ref[top + 8:top + 16, c] * m2
                    e = jnp.concatenate([r1, r2, r1 * m2, jnp.zeros_like(r1)], axis=0)
                    e_hi, e_lo = split(e)
                    u = dot_nn(lhs, jnp.concatenate([e_hi, e_lo, e_hi], axis=0))
                    if q < GR // 16 - 1:
                        r_ref[top + 16:lo_row + GR, c] = r_ref[top + 16:lo_row + GR, c] + u[16:]
                    f_hi, f_lo = split(jnp.concatenate([r1, r2 + m2 * u[8:16]], axis=0))
                    wst_ref[16 * q:16 * q + 16, c] = f_hi
                    wst_ref[GR + 16 * q:GR + 16 * q + 16, c] = f_lo
            later = NOBS - lo_row - GR
            g_hi, g_lo = split(vv_ref[0:XR, rows])
            if later:
                g_hi = jnp.concatenate([sh_ref[lo_row + GR:, rows], g_hi], axis=0)
                g_lo = jnp.concatenate([sl_ref[lo_row + GR:, rows], g_lo], axis=0)
            g_hh = jnp.concatenate([g_hi, g_hi], axis=1)
            for c in wide:
                upd = dot_nn(g_hh, wst_ref[:, c]) + dot_nn(g_lo, wst_ref[0:GR, c])
                if later:
                    r_ref[lo_row + GR:, c] = r_ref[lo_row + GR:, c] + upd[0:later]
                x_ref[0:XR, c] = x_ref[0:XR, c] + upd[later:]
        if t < 2:
            for i in range(4):
                at = (640, 128)[t] + i * 128
                z_ref[i * 128:(i + 1) * 128, :] = x_ref[:, at:at + 128].T
    out_ref[...] = x_ref[:, 0:128]


def vmem():
    return pl.BlockSpec(memory_space=pltpu.VMEM)


def index_call(core, order, device, values, errors):
    return pl.pallas_call(
        index_kernel,
        out_shape=jax.ShapeDtypeStruct((NOBS, 128), F32),
        in_specs=[pl.BlockSpec(memory_space=pltpu.SMEM)] + [vmem()] * 4,
        out_specs=vmem(),
        compiler_params=pltpu.CompilerParams(vmem_limit_bytes=VMEM_LIMIT),
        name="positions",
    )(core, order, device, values, errors)


def main_call(own, other, info, coupling):
    return pl.pallas_call(
        main_kernel,
        out_shape=jax.ShapeDtypeStruct((128, 128), F32),
        in_specs=[vmem()] * 4,
        out_specs=vmem(),
        scratch_shapes=[
            pltpu.VMEM((1024, 384), BF16),
            pltpu.VMEM((NOBS, 128), F32),
            pltpu.VMEM((128, 1152), F32),
            pltpu.VMEM((NOBS, 1152), F32),
            pltpu.VMEM((128, 1152), F32),
            pltpu.VMEM((NOBS, 128), F32),
            pltpu.VMEM((NOBS, 128), F32),
            pltpu.VMEM((NOBS, 128), F32),
            pltpu.VMEM((NOBS, 128), F32),
            pltpu.VMEM((1024, 128), F32),
            pltpu.VMEM((NOBS, 1024), BF16),
            pltpu.VMEM((2 * GR, 1152), BF16),
            pltpu.VMEM((128, NOBS), F32),
            pltpu.VMEM((NOBS, NOBS), BF16),
            pltpu.VMEM((NOBS, NOBS), BF16),
            pltpu.VMEM((GR, 1024), F32),
        ],
        compiler_params=pltpu.CompilerParams(vmem_limit_bytes=VMEM_LIMIT),
        name="filter",
    )(own, other, info, coupling)


def payload_kernel(me_ref, device_ref, cell_ref, flags_ref, ensemble_ref, out_ref,
                   tile_ref, pay_ref, last_ref, sems):
    me = me_ref[0]
    lane = iota((1, NOBS), 1)
    copies, hots = [], []
    lane128 = iota((8, 256), 1)
    for t in range(NB):
        found = jnp.where(device_ref[t:t + 1, :] == me, lane, NOBS)
        one = jnp.min(found)
        two = jnp.min(jnp.where(found == one, NOBS, found))
        for s, pick in enumerate((one, two)):
            at = 2 * t + s
            cell = jnp.max(jnp.where(lane == pick, cell_ref[t:t + 1, :], 0))
            copy = pltpu.make_async_copy(ensemble_ref.at[:, cell >> 8], tile_ref.at[at], sems.at[at])
            copy.start()
            copies.append(copy)
            spot = jnp.where(pick < NOBS, cell & 255, 256)
            hots.append(jnp.where(lane128 == spot, 1.0, 0.0).astype(BF16))
    pay_ref[...] = jnp.zeros_like(pay_ref)
    last_ref[...] = jnp.zeros_like(last_ref)
    for at in range(2 * NB):
        copies[at].wait()
        pair = jnp.concatenate([tile_ref[at, :, 0, :], tile_ref[at, :, 1, :]], axis=1)
        hi, mid = split(pair)
        rest = (pair - hi.astype(F32) - mid.astype(F32)).astype(BF16)
        col = dot_nt(hots[at], hi) + dot_nt(hots[at], mid) + dot_nt(hots[at], rest)
        if at < 5:
            pay_ref[:, 128 * at:128 * at + AUG] = col
        else:
            last_ref[:, 0:AUG] = col
    lane = iota((8, 128), 1)
    last = last_ref[...]
    flags = jnp.broadcast_to(flags_ref[...].astype(F32), (8, 128))
    tails = [pltpu.roll(last, AUG, 1), pltpu.roll(last, AUG - TAIL, 1), pltpu.roll(flags, AUG, 1),
             pltpu.roll(flags, AUG - TAIL, 1), pltpu.roll(flags, (AUG - 2 * TAIL) % 128, 1)]
    for at in range(5):
        row = jnp.where(lane < AUG, pay_ref[:, 128 * at:128 * at + 128], tails[at])
        out_ref[:, 128 * at:128 * at + 128] = jnp.concatenate([row] * 32, axis=0)


def payload_call(me, device, cell, flags, ensemble):
    return pl.pallas_call(
        payload_kernel,
        out_shape=jax.ShapeDtypeStruct((256, PAY), F32),
        in_specs=[pl.BlockSpec(memory_space=pltpu.SMEM)] + [vmem()] * 3 + [pl.BlockSpec(memory_space=pl.ANY)],
        out_specs=vmem(),
        scratch_shapes=[
            pltpu.VMEM((6, AUG, 2, 128), F32),
            pltpu.VMEM((8, PAY), F32),
            pltpu.VMEM((8, 128), F32),
            pltpu.SemaphoreType.DMA((6,)),
        ],
        compiler_params=pltpu.CompilerParams(vmem_limit_bytes=VMEM_LIMIT),
        name="payload",
    )(me, device, cell, flags, ensemble)


def local(ensemble, obs_values, obs_errors, obs_device, obs_cell, obs_order, coupling):
    core = lax.axis_index("c")
    me = ((lax.axis_index("y") * 4 + lax.axis_index("x")) * 2 + core) * 8 + lax.axis_index("z")
    flags = coupling.reshape(1, NB * NBLK)
    payload = payload_call(me.reshape(1), obs_device, obs_cell, flags[:, 0:2 * NBLK], ensemble)
    info = index_call(core.reshape(1), obs_order, obs_device, obs_values, obs_errors)
    own = lax.all_to_all(payload, ("y", "x", "z"), 0, 0, tiled=True)
    other = lax.ppermute(own, "c", [(0, 1), (1, 0)])
    composite = main_call(own, other, info, coupling.reshape(NB, NBLK))
    flat = ensemble.reshape(AUG, -1)
    analysis = jnp.dot(composite[:AUG, :AUG], flat, precision=lax.Precision.HIGH)
    return analysis.reshape(ensemble.shape)


def solution(mesh):
    inner = Mesh(mesh.devices.reshape(8, 4, 2, 8), ("y", "x", "c", "z"))
    state = P(None, None, ("y", "x", "c"), "z")
    placed = (state, P(), P(), P(), P(), P(), state)
    return jax.shard_map(local, mesh=inner, in_specs=placed, out_specs=state, check_vma=False)
```

```python
import functools
import jax
import jax.numpy as jnp
from jax import lax
from jax.experimental import pallas as pl
from jax.experimental.pallas import tpu as pltpu
from jax.sharding import Mesh, PartitionSpec as P

AUG = 81
NB = 3
NOBS = 512
NBLK = 64
OB = 8
PAY = 640
TAIL = 128 - AUG
F32 = jnp.float32
BF16 = jnp.bfloat16
GR = 128
XR = 96
WIDE = 128
VMEM_LIMIT = 56 * 1024 * 1024


def split(x):
    hi = x.astype(BF16)
    lo = (x - hi.astype(F32)).astype(BF16)
    return hi, lo


def dot_nn(a, b):
    return lax.dot_general(a, b, (((1,), (0,)), ((), ())), preferred_element_type=F32)


def dot_nt(a, b):
    return lax.dot_general(a, b, (((1,), (1,)), ((), ())), preferred_element_type=F32)


def iota(shape, dim):
    return lax.broadcasted_iota(jnp.int32, shape, dim)


def index_kernel(core_ref, order_ref, device_ref, values_ref, errors_ref, out_ref):
    core = core_ref[0]
    rows = 128
    lane = iota((rows, NOBS), 1)
    eye = iota((rows, rows), 0) == iota((rows, rows), 1)
    tables = []
    for t in range(NB):
        device = device_ref[t:t + 1, :]
        device_f = device.astype(F32)
        slot = jnp.zeros((1, NOBS), F32)
        for part in range(NOBS // rows):
            sub = iota((rows, NOBS), 0) + part * rows
            own = jnp.sum(jnp.where(eye, device_f[:, part * rows:(part + 1) * rows], 0.0), axis=1, keepdims=True)
            same = jnp.where((own == device_f) & (sub < lane), 1.0, 0.0)
            slot = slot + jnp.sum(same, axis=0, keepdims=True)
        half = ((device >> 3) & 1) ^ core
        place = (device >> 4) * 8 + (device & 7)
        pieces = [half.astype(F32) * 256.0, place.astype(F32), jnp.zeros((1, NOBS), F32)]
        for ref in (values_ref, errors_ref):
            full = ref[t:t + 1, :]
            hi = full.astype(BF16).astype(F32)
            mid = (full - hi).astype(BF16).astype(F32)
            pieces += [hi, mid, full - hi - mid]
        tables.append(jnp.concatenate(pieces + [slot, jnp.zeros((6, NOBS), F32)], axis=0).astype(BF16))
    for part in range(NOBS // rows):
        sub = iota((rows, NOBS), 0) + part * rows
        source = (sub & 63) * OB + (sub >> 6)
        for t in range(NB):
            order = order_ref[t:t + 1, :].astype(F32)
            ident = jnp.sum(jnp.where(source == lane, order, 0.0), axis=1, keepdims=True)
            hot = jnp.where(ident == lane.astype(F32), 1.0, 0.0).astype(BF16)
            got = dot_nt(hot, tables[t])
            out_ref[part * rows:(part + 1) * rows, t * 16:t * 16 + 16] = got
        got = out_ref[part * rows:(part + 1) * rows, :]
        out_ref[part * rows:(part + 1) * rows, :] = got + pltpu.roll(got, 127, 1) + pltpu.roll(got, 126, 1)


def main_kernel(own_ref, other_ref, info_ref, coupling_ref, out_ref,
                buf_ref, z_ref, x_ref, r_ref, mask_ref, w_ref, vt_ref, wk_ref, vk_ref,
                vx_ref, sx_ref, wst_ref, vv_ref, sh_ref, sl_ref, keep_ref):
    lanes = iota((64, 128), 1)
    first = lanes == 0
    valid = lanes < AUG

    for t in range(NB):
        for part, ref in ((0, own_ref), (256, other_ref)):
            if t < 2:
                pieces = [ref[:, 256 * t:256 * t + 128], ref[:, 256 * t + 128:256 * t + 256]]
            else:
                lane = iota((256, 128), 1)
                head = pltpu.roll(ref[:, 0:128], 128 - AUG, 1)
                tail = pltpu.roll(ref[:, 128:256], 256 - 2 * AUG + TAIL - (128 - AUG), 1)
                pieces = [ref[:, 512:640], jnp.where(lane < TAIL, head, tail)]
            for s in range(2):
                hi, lo = split(pieces[s])
                buf_ref[part:part + 256, 256 * s:256 * s + 128] = hi
                buf_ref[part:part + 256, 256 * s + 128:256 * s + 256] = lo
            if t == 0:
                lane = iota((256, 128), 1)
                c0 = pltpu.roll(ref[:, 256:384], 128 - AUG, 1)
                c1 = pltpu.roll(ref[:, 384:512], 128 - AUG + TAIL, 1)
                c2 = pltpu.roll(ref[:, 512:640], (128 - AUG + 2 * TAIL) % 128, 1)
                flags = jnp.where(lane < TAIL, c0, jnp.where(lane < 2 * TAIL, c1, c2)).astype(BF16)
                buf_ref[part:part + 256, 512:640] = flags
        width = 512 if t == 0 else 640
        for i in range(4):
            rows = slice(i * 128, (i + 1) * 128)
            place = info_ref[rows, 16 * t:16 * t + 1].astype(jnp.int32)
            second = info_ref[rows, 16 * t + 9:16 * t + 10] > 0.5
            hot = jnp.where(place == iota((128, 512), 1), 1.0, 0.0).astype(BF16)
            got = dot_nn(hot, buf_ref[:, 0:width])
            z = jnp.where(second, got[:, 256:384] + got[:, 384:512], got[:, 0:128] + got[:, 128:256])
            z = jnp.where(iota((128, 128), 1) < AUG, z, 0.0)
            if t == 0:
                z_ref[rows, :] = z
            else:
                at = (0, 640, 128)[t] + i * 128
                x_ref[:, at:at + 128] = z.T
                mask_ref[:, at:at + 128] = got[:, 512:640].T
    x_ref[:, 0:128] = jnp.where((iota((128, 128), 0) == iota((128, 128), 1))
                                    & (iota((128, 128), 0) < AUG), 1.0, 0.0)

    i0 = iota((GR, 1024), 0)
    i1 = iota((GR, 1024), 1)
    ahead = (i0 >> 4) - (i1 >> 7)
    keep_ref[...] = jnp.where((ahead > 0) | ((ahead == 0) & ((i0 & 15) >= 8) & ((i1 & 31) < 8)), 1.0, 0.0)
    for t in range(NB):
        n = (1152, 640, 128)[t]
        zs = [z_ref[i * 64:(i + 1) * 64, :] for i in range(OB)]
        shrinks, ws = [], []
        hs = [jnp.where(first, 0.0, z) for z in zs]
        gram = [[jnp.sum(hs[j] * hs[l], axis=1, keepdims=True) for l in range(j + 1)] for j in range(OB)]
        cross = [[None] * OB for _ in range(OB)]
        for i in range(OB):
            p = zs[i]
            value = info_ref[i * 64:(i + 1) * 64, 16 * t + 3:16 * t + 4]
            error = info_ref[i * 64:(i + 1) * 64, 16 * t + 6:16 * t + 7]
            h = jnp.where(first, 0.0, p)
            total = gram[i][i]
            q = total / (AUG - 2) + error
            c = 1.0 / ((AUG - 2) * q)
            shrink = c / (1.0 + jnp.sqrt(error / q))
            v = jnp.where(first, c * (value - p[:, 0:1]), -shrink * h)
            v = jnp.where(valid, v, 0.0)
            both = shrink * (2.0 - shrink * total)
            for j in range(i + 1, OB):
                along = gram[j][i]
                zs[j] = zs[j] + v * along
                cross[j][i] = along * (1.0 - shrink * total)
                for l in range(i):
                    cross[j][l] = cross[j][l] - shrink * cross[i][l] * along
                for l in range(i + 1, j + 1):
                    gram[j][l] = gram[j][l] - both * along * gram[l][i]
            w = h
            for l in range(i):
                w = w - ws[l] * (shrinks[l] * cross[i][l])
            shrinks.append(shrink)
            ws.append(w)
            w_ref[i * 64:(i + 1) * 64, :] = w
            vt_ref[i * 64:(i + 1) * 64, :] = v
        for k in range(NBLK):
            wk_ref[k * 8:k * 8 + 8, :] = w_ref[pl.ds(k, 8, stride=64), :]
            vk_ref[k * 8:k * 8 + 8, :] = vt_ref[pl.ds(k, 8, stride=64), :]
        w_hi, w_lo = split(wk_ref[...])
        w_hh = jnp.concatenate([w_hi, w_hi], axis=1)
        for c in range(0, n, 256):
            c = slice(c, min(c + 256, n))
            x_hi, x_lo = split(x_ref[:, c])
            r_ref[:, c] = dot_nn(w_hh, jnp.concatenate([x_hi, x_lo], axis=0)) + dot_nn(w_lo, x_hi)
        for g in range(4):
            vv_ref[:, g * 128:g * 128 + 128] = vk_ref[g * 128:g * 128 + 128, :].T
        own = jnp.sum(jnp.where(iota((64, 64), 0) == iota((64, 64), 1),
                                coupling_ref[t:t + 1, :].astype(F32), 0.0), axis=1, keepdims=True)
        mask_ref[64 * (t % 2):64 * (t % 2) + 64, 0:128] = jnp.broadcast_to(own, (64, 128))

        vk = vk_ref[...]
        v_hi, v_lo = split(vk)
        v_hl = jnp.concatenate([v_hi, v_lo], axis=1)
        groups = [slice(g * GR, g * GR + GR) for g in range(NOBS // GR)]
        bts = [dot_nt(v_hl[r], w_hh[r]) + dot_nt(v_hi[r], w_lo[r]) for r in groups]
        a0 = iota((GR, GR), 0)
        a1 = iota((GR, GR), 1)
        pairs = ((a0 >> 4) == (a1 >> 4)) & ((a0 & 15) < 8) & ((a1 & 15) >= 8)
        v12s = []
        for r, bt in zip(groups, bts):
            b_hi, b_lo = split(jnp.where(pairs, bt, 0.0))
            v12s.append(dot_nn(jnp.concatenate([b_hi, b_hi], axis=1),
                               jnp.concatenate([v_hi[r], v_lo[r]], axis=0)) + dot_nn(b_lo, v_hi[r]))
        for g in range(NOBS // GR - 1):
            r = groups[g]
            s_hi, s_lo = split(dot_nt(w_hh[r.stop:], v_hl[r]) + dot_nt(w_lo[r.stop:], v_hi[r]))
            sh_ref[r.stop:, r] = s_hi
            sl_ref[r.stop:, r] = s_lo
        zero8 = jnp.zeros((8, 128), F32)
        for g, r in enumerate(groups):
            vg, v12 = vk[r], v12s[g]
            for q in range(GR // 16):
                piece = jnp.concatenate([vg[16 * q:16 * q + 8], vg[16 * q + 8:16 * q + 16],
                                         v12[16 * q:16 * q + 8], zero8], axis=0)
                for rep in range(4):
                    vx_ref[q * 128 + rep * 32:q * 128 + rep * 32 + 32, :] = piece
            e_hi, e_lo = split(vx_ref[...])
            sx = dot_nt(w_hh[r], jnp.concatenate([e_hi, e_lo], axis=1)) + dot_nt(w_lo[r], e_hi)
            sx = sx * keep_ref[...]
            s_hi = sx.astype(BF16).astype(F32)
            sx_ref[r, :] = jnp.where((iota((GR, 1024), 1) & 127) < 64, s_hi, sx - s_hi).astype(BF16)

        chunks = [slice(c, min(c + 256, n)) for c in range(0, n, 256)]
        wide = [slice(c, min(c + WIDE, n)) for c in range(0, n, WIDE)]
        for g, rows in enumerate(groups):
            lo_row = g * GR
            for q in range(GR // 16):
                top = lo_row + 16 * q
                mrow = 64 * (t % 2) + top // 8
                lhs = sx_ref[top:lo_row + GR, q * 128:q * 128 + 96]
                for c in chunks:
                    m1 = mask_ref[mrow:mrow + 1, c]
                    m2 = mask_ref[mrow + 1:mrow + 2, c]
                    r1 = r_ref[top:top + 8, c] * m1
                    r2 = r_ref[top + 8:top + 16, c] * m2
                    e = jnp.concatenate([r1, r2, r1 * m2, jnp.zeros_like(r1)], axis=0)
                    e_hi, e_lo = split(e)
                    u = dot_nn(lhs, jnp.concatenate([e_hi, e_lo, e_hi], axis=0))
                    if q < GR // 16 - 1:
                        r_ref[top + 16:lo_row + GR, c] = r_ref[top + 16:lo_row + GR, c] + u[16:]
                    f_hi, f_lo = split(jnp.concatenate([r1, r2 + m2 * u[8:16]], axis=0))
                    wst_ref[16 * q:16 * q + 16, c] = f_hi
                    wst_ref[GR + 16 * q:GR + 16 * q + 16, c] = f_lo
            later = NOBS - lo_row - GR
            g_hi, g_lo = split(vv_ref[0:XR, rows])
            if later:
                g_hi = jnp.concatenate([sh_ref[lo_row + GR:, rows], g_hi], axis=0)
                g_lo = jnp.concatenate([sl_ref[lo_row + GR:, rows], g_lo], axis=0)
            g_hh = jnp.concatenate([g_hi, g_hi], axis=1)
            for c in wide:
                upd = dot_nn(g_hh, wst_ref[:, c]) + dot_nn(g_lo, wst_ref[0:GR, c])
                if later:
                    r_ref[lo_row + GR:, c] = r_ref[lo_row + GR:, c] + upd[0:later]
                x_ref[0:XR, c] = x_ref[0:XR, c] + upd[later:]
        if t < 2:
            for i in range(4):
                at = (640, 128)[t] + i * 128
                z_ref[i * 128:(i + 1) * 128, :] = x_ref[:, at:at + 128].T
    out_ref[...] = x_ref[:, 0:128]


def vmem():
    return pl.BlockSpec(memory_space=pltpu.VMEM)


def index_call(core, order, device, values, errors):
    return pl.pallas_call(
        index_kernel,
        out_shape=jax.ShapeDtypeStruct((NOBS, 128), F32),
        in_specs=[pl.BlockSpec(memory_space=pltpu.SMEM)] + [vmem()] * 4,
        out_specs=vmem(),
        compiler_params=pltpu.CompilerParams(vmem_limit_bytes=VMEM_LIMIT),
        name="positions",
    )(core, order, device, values, errors)


def main_call(own, other, info, coupling):
    return pl.pallas_call(
        main_kernel,
        out_shape=jax.ShapeDtypeStruct((128, 128), F32),
        in_specs=[vmem()] * 4,
        out_specs=vmem(),
        scratch_shapes=[
            pltpu.VMEM((NOBS, 640), BF16),
            pltpu.VMEM((NOBS, 128), F32),
            pltpu.VMEM((128, 1152), F32),
            pltpu.VMEM((NOBS, 1152), F32),
            pltpu.VMEM((128, 1152), F32),
            pltpu.VMEM((NOBS, 128), F32),
            pltpu.VMEM((NOBS, 128), F32),
            pltpu.VMEM((NOBS, 128), F32),
            pltpu.VMEM((NOBS, 128), F32),
            pltpu.VMEM((1024, 128), F32),
            pltpu.VMEM((NOBS, 1024), BF16),
            pltpu.VMEM((2 * GR, 1152), BF16),
            pltpu.VMEM((128, NOBS), F32),
            pltpu.VMEM((NOBS, NOBS), BF16),
            pltpu.VMEM((NOBS, NOBS), BF16),
            pltpu.VMEM((GR, 1024), F32),
        ],
        compiler_params=pltpu.CompilerParams(vmem_limit_bytes=VMEM_LIMIT),
        name="filter",
    )(own, other, info, coupling)


def payload_kernel(me_ref, device_ref, cell_ref, flags_ref, ensemble_ref, out_ref,
                   tile_ref, pay_ref, last_ref, sems):
    me = me_ref[0]
    lane = iota((1, NOBS), 1)
    copies, hots = [], []
    lane128 = iota((8, 256), 1)
    for t in range(NB):
        mine = device_ref[t:t + 1, :] == me
        key = lane * 4096 + cell_ref[t:t + 1, :]
        one = jnp.min(jnp.where(mine, key, NOBS * 4096))
        two = jnp.max(jnp.where(mine, key, -1))
        for s, (pick, held) in enumerate(((one, one < NOBS * 4096), (two, two > one))):
            at = 2 * t + s
            cell = jnp.where(held, pick & 4095, 0)
            copy = pltpu.make_async_copy(ensemble_ref.at[:, cell >> 8], tile_ref.at[at], sems.at[at])
            copy.start()
            copies.append(copy)
            spot = jnp.where(held, cell & 255, 256)
            hots.append(jnp.where(lane128 == spot, 1.0, 0.0).astype(BF16))
    pay_ref[...] = jnp.zeros_like(pay_ref)
    last_ref[...] = jnp.zeros_like(last_ref)
    for at in range(2 * NB):
        copies[at].wait()
        pair = jnp.concatenate([tile_ref[at, :, 0, :], tile_ref[at, :, 1, :]], axis=1)
        hi, mid = split(pair)
        rest = (pair - hi.astype(F32) - mid.astype(F32)).astype(BF16)
        col = dot_nt(hots[at], hi) + dot_nt(hots[at], mid) + dot_nt(hots[at], rest)
        if at < 5:
            pay_ref[:, 128 * at:128 * at + AUG] = col
        else:
            last_ref[:, 0:AUG] = col
    lane = iota((8, 128), 1)
    last = last_ref[...]
    flags = jnp.broadcast_to(flags_ref[...].astype(F32), (8, 128))
    tails = [pltpu.roll(last, AUG, 1), pltpu.roll(last, AUG - TAIL, 1), pltpu.roll(flags, AUG, 1),
             pltpu.roll(flags, AUG - TAIL, 1), pltpu.roll(flags, (AUG - 2 * TAIL) % 128, 1)]
    for at in range(5):
        row = jnp.where(lane < AUG, pay_ref[:, 128 * at:128 * at + 128], tails[at])
        out_ref[:, 128 * at:128 * at + 128] = row


def payload_call(me, device, cell, flags, ensemble):
    return pl.pallas_call(
        payload_kernel,
        out_shape=jax.ShapeDtypeStruct((8, PAY), F32),
        in_specs=[pl.BlockSpec(memory_space=pltpu.SMEM)] + [vmem()] * 3 + [pl.BlockSpec(memory_space=pl.ANY)],
        out_specs=vmem(),
        scratch_shapes=[
            pltpu.VMEM((6, AUG, 2, 128), F32),
            pltpu.VMEM((8, PAY), F32),
            pltpu.VMEM((8, 128), F32),
            pltpu.SemaphoreType.DMA((6,)),
        ],
        compiler_params=pltpu.CompilerParams(vmem_limit_bytes=VMEM_LIMIT),
        name="payload",
    )(me, device, cell, flags, ensemble)


def local(ensemble, obs_values, obs_errors, obs_device, obs_cell, obs_order, coupling):
    core = lax.axis_index("c")
    me = ((lax.axis_index("y") * 4 + lax.axis_index("x")) * 2 + core) * 8 + lax.axis_index("z")
    flags = coupling.reshape(1, NB * NBLK)
    payload = payload_call(me.reshape(1), obs_device, obs_cell, flags[:, 0:2 * NBLK], ensemble)
    info = index_call(core.reshape(1), obs_order, obs_device, obs_values, obs_errors)
    group = lax.axis_size(("y", "x", "z"))
    own = lax.all_to_all(jnp.broadcast_to(payload[0:1], (group, PAY)), ("y", "x", "z"), 0, 0, tiled=True)
    other = lax.ppermute(own, "c", [(0, 1), (1, 0)])
    composite = main_call(own, other, info, coupling.reshape(NB, NBLK))
    flat = ensemble.reshape(AUG, -1)
    analysis = jnp.dot(composite[:AUG, :AUG], flat, precision=lax.Precision.HIGH)
    return analysis.reshape(ensemble.shape)


def solution(mesh):
    inner = Mesh(mesh.devices.reshape(8, 4, 2, 8), ("y", "x", "c", "z"))
    state = P(None, None, ("y", "x", "c"), "z")
    placed = (state, P(), P(), P(), P(), P(), state)
    return jax.shard_map(local, mesh=inner, in_specs=placed, out_specs=state, check_vma=False)
```

```python
import functools
import jax
import jax.numpy as jnp
from jax import lax
from jax.experimental import pallas as pl
from jax.experimental.pallas import tpu as pltpu
from jax.sharding import Mesh, PartitionSpec as P

AUG = 81
NB = 3
NOBS = 512
NBLK = 64
OB = 8
PAY = 640
TAIL = 128 - AUG
F32 = jnp.float32
BF16 = jnp.bfloat16
GR = 128
XR = 96
WIDE = 128
VMEM_LIMIT = 56 * 1024 * 1024


def split(x):
    hi = x.astype(BF16)
    lo = (x - hi.astype(F32)).astype(BF16)
    return hi, lo


def dot_nn(a, b):
    return lax.dot_general(a, b, (((1,), (0,)), ((), ())), preferred_element_type=F32)


def dot_nt(a, b):
    return lax.dot_general(a, b, (((1,), (1,)), ((), ())), preferred_element_type=F32)


def iota(shape, dim):
    return lax.broadcasted_iota(jnp.int32, shape, dim)


def index_kernel(core_ref, order_ref, device_ref, values_ref, errors_ref, out_ref):
    core = core_ref[0]
    rows = 128
    lane = iota((rows, NOBS), 1)
    eye = iota((rows, rows), 0) == iota((rows, rows), 1)
    tables = []
    for t in range(NB):
        device = device_ref[t:t + 1, :]
        device_f = device.astype(F32)
        slot = jnp.zeros((1, NOBS), F32)
        for part in range(NOBS // rows):
            sub = iota((rows, NOBS), 0) + part * rows
            own = jnp.sum(jnp.where(eye, device_f[:, part * rows:(part + 1) * rows], 0.0), axis=1, keepdims=True)
            same = jnp.where((own == device_f) & (sub < lane), 1.0, 0.0)
            slot = slot + jnp.sum(same, axis=0, keepdims=True)
        half = ((device >> 3) & 1) ^ core
        place = (device >> 4) * 8 + (device & 7)
        pieces = [half.astype(F32) * 256.0, place.astype(F32), jnp.zeros((1, NOBS), F32)]
        for ref in (values_ref, errors_ref):
            full = ref[t:t + 1, :]
            hi = full.astype(BF16).astype(F32)
            mid = (full - hi).astype(BF16).astype(F32)
            pieces += [hi, mid, full - hi - mid]
        tables.append(jnp.concatenate(pieces + [slot, jnp.zeros((6, NOBS), F32)], axis=0).astype(BF16))
    for part in range(NOBS // rows):
        sub = iota((rows, NOBS), 0) + part * rows
        source = (sub & 63) * OB + (sub >> 6)
        for t in range(NB):
            order = order_ref[t:t + 1, :].astype(F32)
            ident = jnp.sum(jnp.where(source == lane, order, 0.0), axis=1, keepdims=True)
            hot = jnp.where(ident == lane.astype(F32), 1.0, 0.0).astype(BF16)
            got = dot_nt(hot, tables[t])
            out_ref[part * rows:(part + 1) * rows, t * 16:t * 16 + 16] = got
        got = out_ref[part * rows:(part + 1) * rows, :]
        out_ref[part * rows:(part + 1) * rows, :] = got + pltpu.roll(got, 127, 1) + pltpu.roll(got, 126, 1)


def main_kernel(own_ref, other_ref, info_ref, coupling_ref, out_ref,
                buf_ref, z_ref, x_ref, r_ref, mask_ref, w_ref, vt_ref, wk_ref, vk_ref,
                vx_ref, sx_ref, sy_ref, wst_ref, vv_ref, sh_ref, sl_ref, keep_ref):
    lanes = iota((64, 128), 1)
    first = lanes == 0
    valid = lanes < AUG

    for t in range(NB):
        for part, ref in ((0, own_ref), (256, other_ref)):
            if t < 2:
                pieces = [ref[:, 256 * t:256 * t + 128], ref[:, 256 * t + 128:256 * t + 256]]
            else:
                lane = iota((256, 128), 1)
                head = pltpu.roll(ref[:, 0:128], 128 - AUG, 1)
                tail = pltpu.roll(ref[:, 128:256], 256 - 2 * AUG + TAIL - (128 - AUG), 1)
                pieces = [ref[:, 512:640], jnp.where(lane < TAIL, head, tail)]
            for s in range(2):
                hi, lo = split(pieces[s])
                buf_ref[part:part + 256, 256 * s:256 * s + 128] = hi
                buf_ref[part:part + 256, 256 * s + 128:256 * s + 256] = lo
            if t == 0:
                lane = iota((256, 128), 1)
                c0 = pltpu.roll(ref[:, 256:384], 128 - AUG, 1)
                c1 = pltpu.roll(ref[:, 384:512], 128 - AUG + TAIL, 1)
                c2 = pltpu.roll(ref[:, 512:640], (128 - AUG + 2 * TAIL) % 128, 1)
                flags = jnp.where(lane < TAIL, c0, jnp.where(lane < 2 * TAIL, c1, c2)).astype(BF16)
                buf_ref[part:part + 256, 512:640] = flags
        width = 512 if t == 0 else 640
        for i in range(4):
            rows = slice(i * 128, (i + 1) * 128)
            place = info_ref[rows, 16 * t:16 * t + 1].astype(jnp.int32)
            second = info_ref[rows, 16 * t + 9:16 * t + 10] > 0.5
            hot = jnp.where(place == iota((128, 512), 1), 1.0, 0.0).astype(BF16)
            got = dot_nn(hot, buf_ref[:, 0:width])
            z = jnp.where(second, got[:, 256:384] + got[:, 384:512], got[:, 0:128] + got[:, 128:256])
            z = jnp.where(iota((128, 128), 1) < AUG, z, 0.0)
            if t == 0:
                z_ref[rows, :] = z
            else:
                at = (0, 640, 128)[t] + i * 128
                x_ref[:, at:at + 128] = z.T
                mask_ref[:, at:at + 128] = got[:, 512:640].T
    x_ref[:, 0:128] = jnp.where((iota((128, 128), 0) == iota((128, 128), 1))
                                    & (iota((128, 128), 0) < AUG), 1.0, 0.0)

    i0 = iota((GR, 512), 0)
    i1 = iota((GR, 512), 1)
    ahead = (i0 >> 5) - (i1 >> 7)
    block = (i0 & 31) >> 3
    at = i1 & 127
    inside = ((block >= 1) & (at < 8)) | ((block >= 2) & (at < 24)) \
        | ((block == 3) & ((at < 32) | ((at >= 48) & (at < 72))))
    keep_ref[...] = jnp.where((ahead > 0) | ((ahead == 0) & inside), 1.0, 0.0)
    for t in range(NB):
        n = (1152, 640, 128)[t]
        zs = [z_ref[i * 64:(i + 1) * 64, :] for i in range(OB)]
        shrinks, ws = [], []
        hs = [jnp.where(first, 0.0, z) for z in zs]
        gram = [[jnp.sum(hs[j] * hs[l], axis=1, keepdims=True) for l in range(j + 1)] for j in range(OB)]
        cross = [[None] * OB for _ in range(OB)]
        for i in range(OB):
            p = zs[i]
            value = info_ref[i * 64:(i + 1) * 64, 16 * t + 3:16 * t + 4]
            error = info_ref[i * 64:(i + 1) * 64, 16 * t + 6:16 * t + 7]
            h = jnp.where(first, 0.0, p)
            total = gram[i][i]
            q = total / (AUG - 2) + error
            c = 1.0 / ((AUG - 2) * q)
            shrink = c / (1.0 + jnp.sqrt(error / q))
            v = jnp.where(first, c * (value - p[:, 0:1]), -shrink * h)
            v = jnp.where(valid, v, 0.0)
            both = shrink * (2.0 - shrink * total)
            for j in range(i + 1, OB):
                along = gram[j][i]
                zs[j] = zs[j] + v * along
                cross[j][i] = along * (1.0 - shrink * total)
                for l in range(i):
                    cross[j][l] = cross[j][l] - shrink * cross[i][l] * along
                for l in range(i + 1, j + 1):
                    gram[j][l] = gram[j][l] - both * along * gram[l][i]
            w = h
            for l in range(i):
                w = w - ws[l] * (shrinks[l] * cross[i][l])
            shrinks.append(shrink)
            ws.append(w)
            w_ref[i * 64:(i + 1) * 64, :] = w
            vt_ref[i * 64:(i + 1) * 64, :] = v
        for k in range(NBLK):
            wk_ref[k * 8:k * 8 + 8, :] = w_ref[pl.ds(k, 8, stride=64), :]
            vk_ref[k * 8:k * 8 + 8, :] = vt_ref[pl.ds(k, 8, stride=64), :]
        w_hi, w_lo = split(wk_ref[...])
        w_hh = jnp.concatenate([w_hi, w_hi], axis=1)
        for c in range(0, n, 256):
            c = slice(c, min(c + 256, n))
            x_hi, x_lo = split(x_ref[:, c])
            r_ref[:, c] = dot_nn(w_hh, jnp.concatenate([x_hi, x_lo], axis=0)) + dot_nn(w_lo, x_hi)
        for g in range(4):
            vv_ref[:, g * 128:g * 128 + 128] = vk_ref[g * 128:g * 128 + 128, :].T
        own = jnp.sum(jnp.where(iota((64, 64), 0) == iota((64, 64), 1),
                                coupling_ref[t:t + 1, :].astype(F32), 0.0), axis=1, keepdims=True)
        mask_ref[64 * (t % 2):64 * (t % 2) + 64, 0:128] = jnp.broadcast_to(own, (64, 128))

        vk = vk_ref[...]
        v_hi, v_lo = split(vk)
        v_hl = jnp.concatenate([v_hi, v_lo], axis=1)
        groups = [slice(g * GR, g * GR + GR) for g in range(NOBS // GR)]
        straight = [dot_nt(v_hl[r], w_hh[r]) + dot_nt(v_hi[r], w_lo[r]) for r in groups]
        a0 = iota((GR, GR), 0)
        a1 = iota((GR, GR), 1)
        pairs = ((a0 >> 4) == (a1 >> 4)) & ((a0 & 15) < 8) & ((a1 & 15) >= 8)
        quad = ((a0 >> 5) == (a1 >> 5)) & ((a0 & 31) < 16)
        third = quad & ((a1 & 31) >= 16) & ((a1 & 31) < 24)
        fourth = quad & ((a1 & 31) >= 24)
        v12s, x3s, x4s, x34s = [], [], [], []
        for r, st in zip(groups, straight):
            b_hi, b_lo = split(jnp.where(pairs, st, 0.0))
            v12s.append(dot_nn(jnp.concatenate([b_hi, b_hi], axis=1),
                               jnp.concatenate([v_hi[r], v_lo[r]], axis=0)) + dot_nn(b_lo, v_hi[r]))
        for r, st, v12 in zip(groups, straight, v12s):
            p_hi, p_lo = split(v12)
            bent = dot_nt(jnp.concatenate([p_hi, p_lo], axis=1), w_hh[r]) + dot_nt(p_hi, w_lo[r])
            left = jnp.concatenate([jnp.where(third, st, 0.0), jnp.where(third, bent, 0.0),
                                    jnp.where(fourth, st, 0.0), jnp.where(fourth, bent, 0.0)], axis=0)
            l_hi, l_lo = split(left)
            l_hh = jnp.concatenate([l_hi, l_hi], axis=1)
            x = dot_nn(l_hh, jnp.concatenate([v_hi[r], v_lo[r]], axis=0)) + dot_nn(l_lo, v_hi[r])
            x3s.append((x[0:GR], x[GR:2 * GR]))
            x4s.append((x[2 * GR:3 * GR], x[3 * GR:]))
            x = dot_nn(l_hh[0:2 * GR], jnp.concatenate([p_hi, p_lo], axis=0)) + dot_nn(l_lo[0:2 * GR], p_hi)
            x34s.append((x[0:GR], x[GR:]))
        for g in range(NOBS // GR - 1):
            r = groups[g]
            s_hi, s_lo = split(dot_nt(w_hh[r.stop:], v_hl[r]) + dot_nt(w_lo[r.stop:], v_hi[r]))
            sh_ref[r.stop:, r] = s_hi
            sl_ref[r.stop:, r] = s_lo
        zero8 = jnp.zeros((8, 128), F32)
        for g, r in enumerate(groups):
            vg, v12 = vk[r], v12s[g]
            for q in range(GR // 32):
                at = 32 * q
                vx_ref[128 * q:128 * q + 16, :] = vg[at:at + 16]
                vx_ref[128 * q + 16:128 * q + 24, :] = v12[at:at + 8]
                vx_ref[128 * q + 24:128 * q + 40, :] = vg[at + 16:at + 32]
                vx_ref[128 * q + 40:128 * q + 48, :] = v12[at + 16:at + 24]
                for e, (flat, both) in enumerate((x3s[g], x4s[g], x34s[g])):
                    to = 128 * q + 48 + 24 * e
                    vx_ref[to:to + 16, :] = flat[at:at + 16]
                    vx_ref[to + 16:to + 24, :] = both[at:at + 8]
                vx_ref[128 * q + 120:128 * q + 128, :] = zero8
            e_hi, e_lo = split(vx_ref[...])
            sx = dot_nt(w_hh[r], jnp.concatenate([e_hi, e_lo], axis=1)) + dot_nt(w_lo[r], e_hi)
            s_hi, s_lo = split(sx * keep_ref[...])
            sx_ref[r, :] = s_hi
            sy_ref[r, :] = s_lo

        chunks = [slice(c, min(c + 256, n)) for c in range(0, n, 256)]
        wide = [slice(c, min(c + WIDE, n)) for c in range(0, n, WIDE)]
        for g, rows in enumerate(groups):
            lo_row = g * GR
            for q in range(GR // 32):
                top = lo_row + 32 * q
                mrow = 64 * (t % 2) + top // 8
                s_hi = sx_ref[top:lo_row + GR, q * 128:q * 128 + 128]
                s_hh = jnp.concatenate([s_hi, s_hi], axis=1)
                s_lo = sy_ref[top:lo_row + GR, q * 128:q * 128 + 128]
                for c in chunks:
                    m1, m2, m3, m4 = [mask_ref[mrow + b:mrow + b + 1, c] for b in range(4)]
                    r1, r2, r3, r4 = [r_ref[top + 8 * b:top + 8 * b + 8, c] for b in range(4)]
                    r1 = r1 * m1
                    head = jnp.concatenate([r1, r2 * m2, r1 * m2], axis=0)
                    b3 = r3 * m3
                    by3 = head * m3
                    f = jnp.concatenate([head, b3, r4 * m4, b3 * m4, by3, head * m4, by3 * m4,
                                         jnp.zeros_like(r1)], axis=0)
                    f_hi, f_lo = split(f)
                    u = dot_nn(s_hh, jnp.concatenate([f_hi, f_lo], axis=0)) + dot_nn(s_lo, f_hi)
                    if q < GR // 32 - 1:
                        r_ref[top + 32:lo_row + GR, c] = r_ref[top + 32:lo_row + GR, c] + u[32:]
                    w = jnp.concatenate([r1, (r2 + u[8:16]) * m2, (r3 + u[16:24]) * m3,
                                         (r4 + u[24:32]) * m4], axis=0)
                    f_hi, f_lo = split(w)
                    wst_ref[32 * q:32 * q + 32, c] = f_hi
                    wst_ref[GR + 32 * q:GR + 32 * q + 32, c] = f_lo
            later = NOBS - lo_row - GR
            g_hi, g_lo = split(vv_ref[0:XR, rows])
            if later:
                g_hi = jnp.concatenate([sh_ref[lo_row + GR:, rows], g_hi], axis=0)
                g_lo = jnp.concatenate([sl_ref[lo_row + GR:, rows], g_lo], axis=0)
            g_hh = jnp.concatenate([g_hi, g_hi], axis=1)
            for c in wide:
                upd = dot_nn(g_hh, wst_ref[:, c]) + dot_nn(g_lo, wst_ref[0:GR, c])
                if later:
                    r_ref[lo_row + GR:, c] = r_ref[lo_row + GR:, c] + upd[0:later]
                x_ref[0:XR, c] = x_ref[0:XR, c] + upd[later:]
        if t < 2:
            for i in range(4):
                at = (640, 128)[t] + i * 128
                z_ref[i * 128:(i + 1) * 128, :] = x_ref[:, at:at + 128].T
    out_ref[...] = x_ref[:, 0:128]


def vmem():
    return pl.BlockSpec(memory_space=pltpu.VMEM)


def index_call(core, order, device, values, errors):
    return pl.pallas_call(
        index_kernel,
        out_shape=jax.ShapeDtypeStruct((NOBS, 128), F32),
        in_specs=[pl.BlockSpec(memory_space=pltpu.SMEM)] + [vmem()] * 4,
        out_specs=vmem(),
        compiler_params=pltpu.CompilerParams(vmem_limit_bytes=VMEM_LIMIT),
        name="positions",
    )(core, order, device, values, errors)


def main_call(own, other, info, coupling):
    return pl.pallas_call(
        main_kernel,
        out_shape=jax.ShapeDtypeStruct((128, 128), F32),
        in_specs=[vmem()] * 4,
        out_specs=vmem(),
        scratch_shapes=[
            pltpu.VMEM((NOBS, 640), BF16),
            pltpu.VMEM((NOBS, 128), F32),
            pltpu.VMEM((128, 1152), F32),
            pltpu.VMEM((NOBS, 1152), F32),
            pltpu.VMEM((128, 1152), F32),
            pltpu.VMEM((NOBS, 128), F32),
            pltpu.VMEM((NOBS, 128), F32),
            pltpu.VMEM((NOBS, 128), F32),
            pltpu.VMEM((NOBS, 128), F32),
            pltpu.VMEM((512, 128), F32),
            pltpu.VMEM((NOBS, NOBS), BF16),
            pltpu.VMEM((NOBS, NOBS), BF16),
            pltpu.VMEM((2 * GR, 1152), BF16),
            pltpu.VMEM((128, NOBS), F32),
            pltpu.VMEM((NOBS, NOBS), BF16),
            pltpu.VMEM((NOBS, NOBS), BF16),
            pltpu.VMEM((GR, NOBS), F32),
        ],
        compiler_params=pltpu.CompilerParams(vmem_limit_bytes=VMEM_LIMIT),
        name="filter",
    )(own, other, info, coupling)


def payload_kernel(me_ref, device_ref, cell_ref, flags_ref, ensemble_ref, out_ref,
                   tile_ref, pay_ref, last_ref, sems):
    me = me_ref[0]
    lane = iota((1, NOBS), 1)
    copies, hots = [], []
    lane128 = iota((8, 256), 1)
    for t in range(NB):
        mine = device_ref[t:t + 1, :] == me
        key = lane * 4096 + cell_ref[t:t + 1, :]
        one = jnp.min(jnp.where(mine, key, NOBS * 4096))
        two = jnp.max(jnp.where(mine, key, -1))
        for s, (pick, held) in enumerate(((one, one < NOBS * 4096), (two, two > one))):
            at = 2 * t + s
            cell = jnp.where(held, pick & 4095, 0)
            copy = pltpu.make_async_copy(ensemble_ref.at[:, cell >> 8], tile_ref.at[at], sems.at[at])
            copy.start()
            copies.append(copy)
            spot = jnp.where(held, cell & 255, 256)
            hots.append(jnp.where(lane128 == spot, 1.0, 0.0).astype(BF16))
    pay_ref[...] = jnp.zeros_like(pay_ref)
    last_ref[...] = jnp.zeros_like(last_ref)
    for at in range(2 * NB):
        copies[at].wait()
        pair = jnp.concatenate([tile_ref[at, :, 0, :], tile_ref[at, :, 1, :]], axis=1)
        hi, mid = split(pair)
        rest = (pair - hi.astype(F32) - mid.astype(F32)).astype(BF16)
        col = dot_nt(hots[at], hi) + dot_nt(hots[at], mid) + dot_nt(hots[at], rest)
        if at < 5:
            pay_ref[:, 128 * at:128 * at + AUG] = col
        else:
            last_ref[:, 0:AUG] = col
    lane = iota((8, 128), 1)
    last = last_ref[...]
    flags = jnp.broadcast_to(flags_ref[...].astype(F32), (8, 128))
    tails = [pltpu.roll(last, AUG, 1), pltpu.roll(last, AUG - TAIL, 1), pltpu.roll(flags, AUG, 1),
             pltpu.roll(flags, AUG - TAIL, 1), pltpu.roll(flags, (AUG - 2 * TAIL) % 128, 1)]
    for at in range(5):
        row = jnp.where(lane < AUG, pay_ref[:, 128 * at:128 * at + 128], tails[at])
        out_ref[:, 128 * at:128 * at + 128] = row


def payload_call(me, device, cell, flags, ensemble):
    return pl.pallas_call(
        payload_kernel,
        out_shape=jax.ShapeDtypeStruct((8, PAY), F32),
        in_specs=[pl.BlockSpec(memory_space=pltpu.SMEM)] + [vmem()] * 3 + [pl.BlockSpec(memory_space=pl.ANY)],
        out_specs=vmem(),
        scratch_shapes=[
            pltpu.VMEM((6, AUG, 2, 128), F32),
            pltpu.VMEM((8, PAY), F32),
            pltpu.VMEM((8, 128), F32),
            pltpu.SemaphoreType.DMA((6,)),
        ],
        compiler_params=pltpu.CompilerParams(vmem_limit_bytes=VMEM_LIMIT),
        name="payload",
    )(me, device, cell, flags, ensemble)


def local(ensemble, obs_values, obs_errors, obs_device, obs_cell, obs_order, coupling):
    core = lax.axis_index("c")
    me = ((lax.axis_index("y") * 4 + lax.axis_index("x")) * 2 + core) * 8 + lax.axis_index("z")
    flags = coupling.reshape(1, NB * NBLK)
    payload = payload_call(me.reshape(1), obs_device, obs_cell, flags[:, 0:2 * NBLK], ensemble)
    info = index_call(core.reshape(1), obs_order, obs_device, obs_values, obs_errors)
    group = lax.axis_size(("y", "x", "z"))
    own = lax.all_to_all(jnp.broadcast_to(payload[0:1], (group, PAY)), ("y", "x", "z"), 0, 0, tiled=True)
    other = lax.ppermute(own, "c", [(0, 1), (1, 0)])
    composite = main_call(own, other, info, coupling.reshape(NB, NBLK))
    flat = ensemble.reshape(AUG, -1)
    analysis = jnp.dot(composite[:AUG, :AUG], flat, precision=lax.Precision.HIGH)
    return analysis.reshape(ensemble.shape)


def solution(mesh):
    inner = Mesh(mesh.devices.reshape(8, 4, 2, 8), ("y", "x", "c", "z"))
    state = P(None, None, ("y", "x", "c"), "z")
    placed = (state, P(), P(), P(), P(), P(), state)
    return jax.shard_map(local, mesh=inner, in_specs=placed, out_specs=state, check_vma=False)
```
